32 devices in a mesh: groups: 2 (over y), dp: 4 (over x, core), tensor: 4 (over z).
Axes of the slice: x: 2, y: 2, z: 4, core: 2. Of those that a mesh axis runs over, the one named last changes fastest.
Arguments:
- tokens: bfloat16 [1024, 8192], P(('groups', 'dp'), 'tensor'), parts along dimension 0, may hold values from -6 to 6
- gate_weight: bfloat16 [8192, 16384], P('dp', 'tensor'), may hold values from -0.0625 to 0.0625
- up_weight: bfloat16 [8192, 16384], P('dp', 'tensor'), may hold values from -0.0625 to 0.0625
- down_weight: bfloat16 [16384, 8192], P('tensor', 'dp'), may hold values from -0.0625 to 0.0625
- block_ids: int32 [256], P(('groups', 'tensor')), parts along dimension 0, may hold values from 0 to 127, as said below
- block_counts: int32 [8], P(('groups', 'tensor')), parts along dimension 0, may hold values from 1 to 32
Outputs:
- mixed: bfloat16 [1024, 8192], P(('groups', 'dp'), 'tensor'), parts along dimension 0
The draws below stay inside these ranges and needn't reach their ends.
There are 2 independent parts, one for each index of `groups`. The reference program is written for one: setup_inputs(seed, part) draws one part's arguments, and reference() takes and returns one part's arrays. A program takes and returns all parts, laid end to end along the dimension named above; an argument that names none is the same for every part. Nothing has to cross between parts.
Inputs may be any that keep to these rules, and one draw needn't show every extreme that they name: `block_ids`: each shard's 32 entries name that shard's own blocks, each once; entries past the shard's count are padding.
All inputs are finite; a program needn't handle non-finite values.
Results may differ from the reference program's by a relative error of at most 0.005.
Values may be sent and summed in bfloat16 or wider, within the bound.
No kernel may reach another device: no remote copies, remote signals or barrier semaphores. Data moves between devices by JAX's collectives and lax.ppermute only.
A program may use at most 512 MiB of HBM per device.

```python
import jax
import jax.numpy as jnp

D = 8192
FF = 16384
BLOCK = 128
ROWS = 512
NBLK = 128
BLK_DEV = 32


def draw_block_ids(key, part):
    key = jax.random.fold_in(key, 11)
    shards = NBLK // BLK_DEV
    subkeys = jax.random.split(key, shards)
    orders = jax.vmap(lambda sub: jax.random.permutation(sub, BLK_DEV))(subkeys)
    owners = jnp.arange(shards, dtype=jnp.int32)[:, None] * BLK_DEV
    return (orders.astype(jnp.int32) + owners).reshape(NBLK)


def draw_block_counts(key, part):
    key = jax.random.fold_in(key, 12)
    shards = NBLK // BLK_DEV
    counts = jax.random.randint(key, (shards,), 1, BLK_DEV + 1, dtype=jnp.int32)
    counts = counts.at[0].set(BLK_DEV)
    return counts.at[1].set(1)


def raised(entries, rng, source, target, blocks, factor):
    owner, partner = [(jnp.arange(entries.shape[dim]) // (entries.shape[dim] // blocks)).reshape([-1 if axis == dim else 1 for axis in range(entries.ndim)]) for dim in (source, target)]
    chosen = jax.random.permutation(rng, blocks)[partner]
    strong = (owner == chosen) | (owner == (partner + blocks // 2) % blocks)
    return jnp.where(strong, factor * entries, entries)


def level_of(own_key, dims, cuts, low, largest):
    loudness, own = 1.0, jax.random.fold_in(own_key, 6)
    for axis_at, parts in cuts:
        heights = jnp.exp(jax.random.uniform(jax.random.fold_in(own, axis_at), (parts,), jnp.float32, low / len(cuts), largest / len(cuts)))
        loudness = loudness * jnp.repeat(heights, dims[axis_at] // parts).reshape([-1 if axis == axis_at else 1 for axis in range(len(dims))])
    return loudness


def centred(stream_key, dims, scale, reach, cuts=(), held_as=jnp.bfloat16):
    drawn = jax.random.normal(stream_key, dims, jnp.float32) * scale
    if len(cuts) > 0:
        drawn = level_of(stream_key, dims, cuts, -0.22, 0.18) * drawn
    return jnp.clip(drawn, min=-reach, max=reach).astype(held_as)


def bell_draw_with(stream_key, dims, deviation, reach, pieces, heavy, held_as=jnp.bfloat16):
    drawn = deviation * jax.random.normal(stream_key, dims, jnp.float32)
    if pieces:
        drawn = drawn * level_of(stream_key, dims, pieces, -0.22, 0.18)
    return jnp.clip(raised(drawn, jax.random.fold_in(stream_key, 3), *heavy), -reach, reach).astype(held_as)


def setup_inputs(seed: int = 0, part: int = 0) -> dict:
    streams_of = jax.random.split(jax.random.key(seed), 7)
    own_keys = jax.random.split(jax.random.fold_in(streams_of[6], part), 7)
    tokens = centred(own_keys[0], (ROWS, D), 1.0, 6.0, ((0, 4), (1, 4)))
    gate_weight = centred(streams_of[1], (D, FF), D ** -0.5, 0.0625, ((0, 4), (1, 4)))
    up_weight = centred(streams_of[2], (D, FF), D ** -0.5, 0.0625, ((0, 4), (1, 4)))
    down_weight = bell_draw_with(streams_of[3], (FF, D), FF ** -0.5, 0.0625, ((0, 4), (1, 4)), (0, 1, 4, 2.0))
    block_ids = draw_block_ids(jax.random.fold_in(jax.random.fold_in(streams_of[6], part), 71), part)
    block_counts = draw_block_counts(jax.random.fold_in(jax.random.fold_in(streams_of[6], part), 71), part)
    return {"tokens": tokens, "gate_weight": gate_weight, "up_weight": up_weight, "down_weight": down_weight, "block_ids": block_ids, "block_counts": block_counts}


def reference(tokens, gate_weight, up_weight, down_weight, block_ids, block_counts):
    gate_sum = jnp.dot(tokens, gate_weight, preferred_element_type=jnp.float32)
    up_sum = jnp.dot(tokens, up_weight, preferred_element_type=jnp.float32)
    shards = NBLK // BLK_DEV
    local_ids = block_ids.reshape(shards, BLK_DEV) % BLK_DEV
    places = jnp.arange(BLK_DEV, dtype=jnp.int32)
    in_count = places[None, :] < block_counts[:, None]
    match = (local_ids[:, :, None] == places[None, None, :]) & in_count[:, :, None]
    active = jnp.any(match, axis=1).astype(jnp.float32).reshape(NBLK)
    unit_mask = jnp.repeat(active, BLOCK)
    hidden = (jnp.maximum(gate_sum, 0.0) * up_sum * unit_mask[None, :]).astype(jnp.bfloat16)
    return jnp.dot(hidden, down_weight, preferred_element_type=jnp.float32).astype(jnp.bfloat16)
```

```python
import functools

import jax
import jax.numpy as jnp
from jax import lax
from jax.experimental import pallas as pl
from jax.experimental.pallas import tpu as pltpu
from jax.sharding import PartitionSpec as P

CHUNKS = 2
BF16, F32 = jnp.bfloat16, jnp.float32


def xor_perm(size, mask):
    return [(i, i ^ mask) for i in range(size)]


def active_units(block_ids, block_counts, unit_count):
    block_total = block_ids.shape[0]
    places = jnp.arange(block_total, dtype=jnp.int32)
    match = (block_ids[:, None] % block_total == places[None, :]) & (
        places < block_counts[0]
    )[:, None]
    active = jnp.any(match, axis=0).astype(F32)
    return jnp.repeat(active, unit_count // block_total)


def gate_up_kernel(td_ref, x0, x1, x2, x3, gate_ref, up_ref, keep_ref, send_ref, xs):
    rows = x0.shape[0]

    @pl.when(pl.program_id(0) == 0)
    def _():
        for j, x in enumerate((x0, x1, x2, x3)):
            place = pl.multiple_of((j ^ td_ref[0]) * rows, rows)
            xs[pl.ds(place, rows), :] = x[...]

    for i, w in enumerate((gate_ref, up_ref)):
        acc = jnp.dot(xs[...], w[...], preferred_element_type=F32)
        keep_ref[0, i] = acc[:rows]
        send_ref[0, i] = acc[rows : 2 * rows].astype(BF16)
        keep_ref[1, i] = acc[2 * rows : 3 * rows]
        send_ref[1, i] = acc[3 * rows :].astype(BF16)


def gate_up(td, blocks, gate_weight, up_weight, tile=512):
    rows, depth = blocks[0].shape
    units = gate_weight.shape[1]
    whole = pl.BlockSpec((rows, depth), lambda i, td: (0, 0))
    part = pl.BlockSpec((depth, tile), lambda i, td: (0, i))
    out = pl.BlockSpec((2, 2, rows, tile), lambda i, td: (0, 0, 0, i))
    return pl.pallas_call(
        gate_up_kernel,
        grid_spec=pltpu.PrefetchScalarGridSpec(
            num_scalar_prefetch=1,
            grid=(units // tile,),
            in_specs=[whole] * 4 + [part] * 2,
            out_specs=[out, out],
            scratch_shapes=[pltpu.VMEM((4 * rows, depth), BF16)],
        ),
        out_shape=[
            jax.ShapeDtypeStruct((2, 2, rows, units), F32),
            jax.ShapeDtypeStruct((2, 2, rows, units), BF16),
        ],
        compiler_params=pltpu.CompilerParams(vmem_limit_bytes=40 << 20),
        cost_estimate=pl.CostEstimate(
            flops=16 * rows * depth * units,
            bytes_accessed=4 * depth * units + 8 * rows * depth + 24 * rows * units,
            transcendentals=0,
        ),
        name="gate_up",
    )(td, *blocks, gate_weight, up_weight)


def down_kernel(td_ref, h0, h2, h13, down_ref, o0, o1, o2, o3, hs):
    rows = h0.shape[0]

    @pl.when(pl.program_id(0) == 0)
    def _():
        for k in range(4):
            place = pl.multiple_of((k ^ td_ref[0]) * rows, rows)
            h = h0[...] if k == 0 else h2[...] if k == 2 else h13[k // 2]
            hs[pl.ds(place, rows), :] = h

    acc = jnp.dot(hs[...], down_ref[...], preferred_element_type=F32)
    for j, o in enumerate((o0, o1, o2, o3)):
        o[...] = acc[j * rows : (j + 1) * rows].astype(o.dtype)


def down(td, h0, h2, h13, down_weight, tile=256):
    rows, depth = h0.shape
    width = down_weight.shape[1]
    whole = pl.BlockSpec((rows, depth), lambda i, td: (0, 0))
    pair = pl.BlockSpec((2, rows, depth), lambda i, td: (0, 0, 0))
    part = pl.BlockSpec((depth, tile), lambda i, td: (0, i))
    out = pl.BlockSpec((rows, tile), lambda i, td: (0, i))
    return pl.pallas_call(
        down_kernel,
        grid_spec=pltpu.PrefetchScalarGridSpec(
            num_scalar_prefetch=1,
            grid=(width // tile,),
            in_specs=[whole, whole, pair, part],
            out_specs=[out] * 4,
            scratch_shapes=[pltpu.VMEM((4 * rows, depth), BF16)],
        ),
        out_shape=[jax.ShapeDtypeStruct((rows, width), t) for t in (F32, BF16, BF16, BF16)],
        compiler_params=pltpu.CompilerParams(vmem_limit_bytes=40 << 20),
        cost_estimate=pl.CostEstimate(
            flops=8 * rows * depth * width,
            bytes_accessed=2 * depth * width + 8 * rows * depth + 10 * rows * width,
            transcendentals=0,
        ),
        name="down",
    )(td, h0, h2, h13, down_weight)


def per_device(tokens, gate_weight, up_weight, down_weight, block_ids, block_counts):
    d, t = lax.axis_index("dp"), lax.axis_index("tensor")
    td = (d ^ t).reshape(1).astype(jnp.int32)
    active = active_units(block_ids, block_counts, gate_weight.shape[1])
    turn = [(a * 4 + b, b * 4 + a) for a in range(4) for b in range(4)]
    rows = tokens.shape[0] // CHUNKS
    swap = lambda x, axis, mask: lax.ppermute(x, axis, xor_perm(4, mask))
    outs = []
    for c in range(CHUNKS):
        mine = lax.ppermute(tokens[c * rows : (c + 1) * rows], ("dp", "tensor"), turn)
        blocks = [mine] + [swap(mine, "tensor", j) for j in (1, 2, 3)]
        keep, send = gate_up(td, blocks, gate_weight, up_weight)
        near = swap(send, "dp", 1)
        across = swap((keep[1] + near[1].astype(F32)).astype(BF16), "dp", 2)
        total = keep[0] + near[0].astype(F32) + across.astype(F32)
        hidden = (jnp.maximum(total[0], 0.0) * total[1] * active).astype(BF16)
        far = swap(hidden, "dp", 2)
        other = swap(jnp.stack([hidden, far]), "dp", 1)
        o = down(td, hidden, far, other, down_weight)
        mixed = o[0]
        for j in (1, 2, 3):
            mixed = mixed + swap(o[j], "tensor", j).astype(F32)
        outs.append(lax.ppermute(mixed.astype(BF16), ("dp", "tensor"), turn))
    return jnp.concatenate(outs, axis=0)


def per_device_general(tokens, gate_weight, up_weight, down_weight, block_ids, block_counts):
    gathered = lax.all_gather(tokens, "tensor", axis=1, tiled=True)
    turned = lax.all_to_all(gathered, "dp", 1, 0, tiled=True)
    active = active_units(block_ids, block_counts, gate_weight.shape[1])
    sums = [
        lax.psum_scatter(
            jnp.dot(turned, w, preferred_element_type=F32), "dp", scatter_dimension=0, tiled=True
        )
        for w in (gate_weight, up_weight)
    ]
    hidden = (jnp.maximum(sums[0], 0.0) * sums[1] * active).astype(BF16)
    hidden = lax.all_gather(hidden, "dp", axis=0, tiled=True)
    partial = jnp.dot(hidden, down_weight, preferred_element_type=F32)
    partial = lax.all_to_all(partial, "dp", 0, 1, tiled=True)
    return lax.psum_scatter(partial, "tensor", scatter_dimension=1, tiled=True).astype(BF16)


def solution(mesh):
    placed = (
        P(("groups", "dp"), "tensor"),
        P("dp", "tensor"),
        P("dp", "tensor"),
        P("tensor", "dp"),
        P(("groups", "tensor")),
        P(("groups", "tensor")),
    )
    square = mesh.shape["dp"] == 4 and mesh.shape["tensor"] == 4
    return jax.shard_map(
        per_device if square else per_device_general,
        mesh=mesh,
        in_specs=placed,
        out_specs=P(("groups", "dp"), "tensor"),
        check_vma=False,
    )
```

```python
import functools

import jax
import jax.numpy as jnp
from jax import lax
from jax.experimental import pallas as pl
from jax.experimental.pallas import tpu as pltpu
from jax.sharding import PartitionSpec as P

SIZES = (64, 64)
CHUNKS = len(SIZES)
COST1 = 20000
COST2 = 1000
HOLD = True
AFTER = True
SPREAD = "p"
HALVES = (1, 1)
MIXAT = 1
TILE2 = 512
CUBE = (True, True)
ORDER = 0
MIX = 0
RESIDENT = False
BF16, F32 = jnp.bfloat16, jnp.float32


def xor_perm(size, mask):
    return [(i, i ^ mask) for i in range(size)]


def active_units(block_ids, block_counts, unit_count):
    block_total = block_ids.shape[0]
    places = jnp.arange(block_total, dtype=jnp.int32)
    match = (block_ids[:, None] % block_total == places[None, :]) & (
        places < block_counts[0]
    )[:, None]
    active = jnp.any(match, axis=0).astype(F32)
    return jnp.repeat(active, unit_count // block_total)


def gate_up_kernel(tile, td_ref, *refs):
    xrefs, (gate_ref, up_ref, keep_ref, send_ref, xs) = refs[:-5], refs[-5:]
    rows = xs.shape[0] // 4

    @pl.when(pl.program_id(0) == 0)
    def _():
        for j in range(4):
            place = pl.multiple_of((j ^ td_ref[0]) * rows, rows)
            xs[pl.ds(place, rows), :] = xrefs[j][...] if len(xrefs) == 4 else xrefs[0][j]

    cols = pl.ds(pl.multiple_of(pl.program_id(0) * tile, tile), tile)
    for i, w in enumerate((gate_ref, up_ref)):
        acc = jnp.dot(xs[...], w[:, cols] if RESIDENT else w[...], preferred_element_type=F32)
        keep_ref[0, i] = acc[:rows]
        send_ref[0, i] = acc[rows : 2 * rows].astype(BF16)
        keep_ref[1, i] = acc[2 * rows : 3 * rows]
        send_ref[1, i] = acc[3 * rows :].astype(BF16)


def gate_up(td, blocks, gate_weight, up_weight, tile=512):
    rows, depth = blocks[0].shape[-2:]
    units = gate_weight.shape[1]
    whole = [pl.BlockSpec(x.shape, lambda i, td, r=x.ndim: (0,) * r) for x in blocks]
    part = pl.BlockSpec(memory_space=pltpu.VMEM) if RESIDENT else pl.BlockSpec((depth, tile), lambda i, td: (0, i))
    out = pl.BlockSpec((2, 2, rows, tile), lambda i, td: (0, 0, 0, i))
    return pl.pallas_call(
        functools.partial(gate_up_kernel, tile),
        grid_spec=pltpu.PrefetchScalarGridSpec(
            num_scalar_prefetch=1,
            grid=(units // tile,),
            in_specs=whole + [part] * 2,
            out_specs=[out, out],
            scratch_shapes=[pltpu.VMEM((4 * rows, depth), BF16)],
        ),
        out_shape=[
            jax.ShapeDtypeStruct((2, 2, rows, units), F32),
            jax.ShapeDtypeStruct((2, 2, rows, units), BF16),
        ],
        compiler_params=pltpu.CompilerParams(vmem_limit_bytes=(8 if RESIDENT else 40) << 20),
        cost_estimate=pl.CostEstimate(
            flops=COST1 * 1000,
            bytes_accessed=COST1 * 1000,
            transcendentals=0,
        ),
        name="gate_up",
    )(td, *blocks, gate_weight, up_weight)


def down_kernel(tile, td_ref, h0, h1, h2, h3, down_ref, own_ref, full_ref, hs):
    rows = h0.shape[0]

    @pl.when(pl.program_id(0) == 0)
    def _():
        for k, h in enumerate((h0, h1, h2, h3)):
            place = pl.multiple_of((k ^ td_ref[0]) * rows, rows)
            hs[pl.ds(place, rows), :] = h[...]

    cols = pl.ds(pl.multiple_of(pl.program_id(0) * tile, tile), tile)
    acc = jnp.dot(hs[...], down_ref[:, cols] if RESIDENT else down_ref[...], preferred_element_type=F32)
    own_ref[...] = acc[:rows]
    for j in range(4):
        full_ref[j ^ td_ref[1]] = acc[j * rows : (j + 1) * rows].astype(BF16)


def down(td, h0, h1, h2, h3, down_weight, part, parts):
    rows, depth = h0.shape
    width = down_weight.shape[1] // parts
    tile = TILE2
    first = part * (width // tile)
    whole = pl.BlockSpec((rows, depth), lambda i, td: (0, 0))
    weight = pl.BlockSpec((depth, tile), lambda i, td: (0, first + i))
    out = pl.BlockSpec((rows, tile), lambda i, td: (0, i))
    return pl.pallas_call(
        functools.partial(down_kernel, tile),
        grid_spec=pltpu.PrefetchScalarGridSpec(
            num_scalar_prefetch=1,
            grid=(width // tile,),
            in_specs=[whole] * 4 + [weight],
            out_specs=[out, pl.BlockSpec((4, rows, tile), lambda i, td: (0, 0, i))],
            scratch_shapes=[pltpu.VMEM((4 * rows, depth), BF16)],
        ),
        out_shape=[jax.ShapeDtypeStruct((rows, width), F32), jax.ShapeDtypeStruct((4, rows, width), BF16)],
        compiler_params=pltpu.CompilerParams(vmem_limit_bytes=(8 if RESIDENT else 40) << 20),
        cost_estimate=pl.CostEstimate(
            flops=COST2 * 1000,
            bytes_accessed=COST2 * 1000,
            transcendentals=0,
        ),
        name="down",
    )(td, h0, h1, h2, h3, down_weight)


def per_device(tokens, gate_weight, up_weight, down_weight, block_ids, block_counts):
    d, t = lax.axis_index("dp"), lax.axis_index("tensor")
    td = (d ^ t).reshape(1).astype(jnp.int32)
    dt = jnp.stack([d ^ t, t]).astype(jnp.int32)
    dd = d.reshape(1).astype(jnp.int32)
    active = active_units(block_ids, block_counts, gate_weight.shape[1])
    turn = [(a * 4 + b, b * 4 + a) for a in range(4) for b in range(4)]
    starts = [sum(SIZES[:c]) for c in range(CHUNKS + 1)]
    swap = lambda x, axis, mask: lax.ppermute(x, axis, xor_perm(4, mask))
    after = lambda x, *earlier: lax.optimization_barrier((x, *earlier))[0]
    blocks, mine, keep, send, near, across, hidden, far, pair = ([None] * CHUNKS for _ in range(9))
    parts, got, outs = {}, {}, {}
    tick = [td]


    def turn_in(c):
        x = tokens[starts[c] : starts[c + 1]]
        if c > 0:
            x = after(x, mine[c - 1])
        mine[c] = lax.ppermute(x, ("dp", "tensor"), turn)

    def spread(c):
        x = mine[c]
        if c > 0 and AFTER:
            x = after(x, *blocks[c - 1])
        if SPREAD == "a":
            y = lax.all_to_all(jnp.broadcast_to(x, (4, *x.shape)), "tensor", 0, 0, tiled=True)
            blocks[c] = [y]
        else:
            one, two = swap(x, "tensor", 1), swap(x, "tensor", 2)
            three = swap(two, "tensor", 1) if CUBE[c] else swap(x, "tensor", 3)
            blocks[c] = [mine[c], one, two, three]

    def first(c):
        if c + 1 < CHUNKS:
            tick.append(mine[c + 1])
        keep[c], send[c] = gate_up(after(dd if SPREAD == "a" else td, *tick), blocks[c], gate_weight, up_weight)
        tick[:] = [send[c]]

    def near_sum(c):
        held = after(send[c], *blocks[c + 1][:3 if CUBE[c + 1] else 4]) if HOLD and c + 1 < CHUNKS else send[c]
        near[c] = swap(held, "dp", 1)

    def add(c):
        x, _ = lax.optimization_barrier((keep[c], tuple(tick)))
        keep[c] = x
        summed = (x[1] + near[c][1].astype(F32)).astype(BF16)
        across[c] = swap(summed, "dp", 2)
        tick[:] = [summed]

    def gated(c):
        x, _ = lax.optimization_barrier((keep[c], tuple(tick)))
        total = x[0] + near[c][0].astype(F32) + across[c].astype(F32)
        hidden[c] = (jnp.maximum(total[0], 0.0) * total[1] * active).astype(BF16)
        far[c] = swap(hidden[c], "dp", 2)
        pair[c] = [swap(hidden[c], "dp", 1), swap(far[c], "dp", 1)]
        tick[:] = [hidden[c]]

    def second(c, h):
        parts[c, h] = down(after(dt, *tick), hidden[c], pair[c][0], far[c], pair[c][1], down_weight, h, HALVES[c])
        got[c, h] = lax.all_to_all(parts[c, h][1], "tensor", 0, 0, tiled=True)
        tick[:] = [parts[c, h][1]]

    def mix(c, h):
        mixed, _ = lax.optimization_barrier((parts[c, h][0], tuple(tick)))
        for j in range(4):
            mixed = mixed + jnp.where(t == j, 0.0, got[c, h][j].astype(F32))
        mixed = mixed.astype(BF16)
        outs[c, h] = lax.ppermute(mixed, ("dp", "tensor"), turn)
        tick[:] = [mixed]

    turn_in(0)
    spread(0)
    turn_in(1)
    first(0)
    spread(1)
    near_sum(0)
    add(0)
    first(1)
    near_sum(1)
    gated(0)
    add(1)
    for h in range(HALVES[0]):
        second(0, h)
    gated(1)
    second(1, 0)
    if MIXAT == 0:
        for h in range(HALVES[0]):
            mix(0, h)
    for h in range(1, HALVES[1]):
        second(1, h)
    if MIXAT == 1:
        for h in range(HALVES[0]):
            mix(0, h)
    for h in range(HALVES[1]):
        mix(1, h)
    return jnp.concatenate(
        [jnp.concatenate([outs[c, h] for h in range(HALVES[c])], axis=1) for c in range(CHUNKS)], axis=0
    )


def per_device_general(tokens, gate_weight, up_weight, down_weight, block_ids, block_counts):
    gathered = lax.all_gather(tokens, "tensor", axis=1, tiled=True)
    turned = lax.all_to_all(gathered, "dp", 1, 0, tiled=True)
    active = active_units(block_ids, block_counts, gate_weight.shape[1])
    sums = [
        lax.psum_scatter(
            jnp.dot(turned, w, preferred_element_type=F32), "dp", scatter_dimension=0, tiled=True
        )
        for w in (gate_weight, up_weight)
    ]
    hidden = (jnp.maximum(sums[0], 0.0) * sums[1] * active).astype(BF16)
    hidden = lax.all_gather(hidden, "dp", axis=0, tiled=True)
    partial = jnp.dot(hidden, down_weight, preferred_element_type=F32)
    partial = lax.all_to_all(partial, "dp", 0, 1, tiled=True)
    return lax.psum_scatter(partial, "tensor", scatter_dimension=1, tiled=True).astype(BF16)


def solution(mesh):
    placed = (
        P(("groups", "dp"), "tensor"),
        P("dp", "tensor"),
        P("dp", "tensor"),
        P("tensor", "dp"),
        P(("groups", "tensor")),
        P(("groups", "tensor")),
    )
    square = mesh.shape["dp"] == 4 and mesh.shape["tensor"] == 4
    return jax.shard_map(
        per_device if square else per_device_general,
        mesh=mesh,
        in_specs=placed,
        out_specs=P(("groups", "dp"), "tensor"),
        check_vma=False,
    )
```

```python
import functools

import jax
import jax.numpy as jnp
from jax import lax
from jax.experimental import pallas as pl
from jax.experimental.pallas import tpu as pltpu
from jax.sharding import PartitionSpec as P

SIZES = (64, 64)
CHUNKS = len(SIZES)
COST1 = 20000
COST2 = 1000
HOLD = True
AFTER = True
SPREAD = "p"
HALVES = (1, 2)
MIXAT = 0
MODE = ("a", "x")
TILE2 = 512
TILE1 = 1024
HOLD2 = False
CUBE = (True, True)
ORDER = 0
MIX = 0
RESIDENT = False
BF16, F32 = jnp.bfloat16, jnp.float32


def xor_perm(size, mask):
    return [(i, i ^ mask) for i in range(size)]


def active_units(block_ids, block_counts, unit_count):
    block_total = block_ids.shape[0]
    places = jnp.arange(block_total, dtype=jnp.int32)
    match = (block_ids[:, None] % block_total == places[None, :]) & (
        places < block_counts[0]
    )[:, None]
    active = jnp.any(match, axis=0).astype(F32)
    return jnp.repeat(active, unit_count // block_total)


def gate_up_kernel(tile, td_ref, *refs):
    xrefs, (gate_ref, up_ref, keep_ref, send_ref, xs) = refs[:-5], refs[-5:]
    rows = xs.shape[0] // 4

    @pl.when(pl.program_id(0) == 0)
    def _():
        for j in range(4):
            place = pl.multiple_of((j ^ td_ref[0]) * rows, rows)
            xs[pl.ds(place, rows), :] = xrefs[j][...] if len(xrefs) == 4 else xrefs[0][j]

    cols = pl.ds(pl.multiple_of(pl.program_id(0) * tile, tile), tile)
    for i, w in enumerate((gate_ref, up_ref)):
        acc = jnp.dot(xs[...], w[:, cols] if RESIDENT else w[...], preferred_element_type=F32)
        keep_ref[0, i] = acc[:rows]
        send_ref[0, i] = acc[rows : 2 * rows].astype(BF16)
        keep_ref[1, i] = acc[2 * rows : 3 * rows]
        send_ref[1, i] = acc[3 * rows :].astype(BF16)


def gate_up(td, blocks, gate_weight, up_weight):
    tile = TILE1
    rows, depth = blocks[0].shape[-2:]
    units = gate_weight.shape[1]
    whole = [pl.BlockSpec(x.shape, lambda i, td, r=x.ndim: (0,) * r) for x in blocks]
    part = pl.BlockSpec(memory_space=pltpu.VMEM) if RESIDENT else pl.BlockSpec((depth, tile), lambda i, td: (0, i))
    out = pl.BlockSpec((2, 2, rows, tile), lambda i, td: (0, 0, 0, i))
    return pl.pallas_call(
        functools.partial(gate_up_kernel, tile),
        grid_spec=pltpu.PrefetchScalarGridSpec(
            num_scalar_prefetch=1,
            grid=(units // tile,),
            in_specs=whole + [part] * 2,
            out_specs=[out, out],
            scratch_shapes=[pltpu.VMEM((4 * rows, depth), BF16)],
        ),
        out_shape=[
            jax.ShapeDtypeStruct((2, 2, rows, units), F32),
            jax.ShapeDtypeStruct((2, 2, rows, units), BF16),
        ],
        compiler_params=pltpu.CompilerParams(vmem_limit_bytes=(8 if RESIDENT else 40) << 20),
        cost_estimate=pl.CostEstimate(
            flops=COST1 * 1000,
            bytes_accessed=COST1 * 1000,
            transcendentals=0,
        ),
        name="gate_up",
    )(td, *blocks, gate_weight, up_weight)


def down_kernel(tile, td_ref, h0, h1, h2, h3, down_ref, own_ref, *refs):
    outs, hs = refs[:-1], refs[-1]
    rows = h0.shape[0]

    @pl.when(pl.program_id(0) == 0)
    def _():
        for k, h in enumerate((h0, h1, h2, h3)):
            place = pl.multiple_of((k ^ td_ref[0]) * rows, rows)
            hs[pl.ds(place, rows), :] = h[...]

    cols = pl.ds(pl.multiple_of(pl.program_id(0) * tile, tile), tile)
    acc = jnp.dot(hs[...], down_ref[:, cols] if RESIDENT else down_ref[...], preferred_element_type=F32)
    own_ref[...] = acc[:rows]
    if len(outs) == 1:
        for j in range(4):
            outs[0][j ^ td_ref[1]] = acc[j * rows : (j + 1) * rows].astype(BF16)
    else:
        for j in (1, 2, 3):
            outs[j - 1][...] = acc[j * rows : (j + 1) * rows].astype(BF16)


def down(td, h0, h1, h2, h3, down_weight, part, parts, mode):
    rows, depth = h0.shape
    width = down_weight.shape[1] // parts
    tile = TILE2
    first = part * (width // tile)
    whole = pl.BlockSpec((rows, depth), lambda i, td: (0, 0))
    weight = pl.BlockSpec((depth, tile), lambda i, td: (0, first + i))
    out = pl.BlockSpec((rows, tile), lambda i, td: (0, i))
    return pl.pallas_call(
        functools.partial(down_kernel, tile),
        grid_spec=pltpu.PrefetchScalarGridSpec(
            num_scalar_prefetch=1,
            grid=(width // tile,),
            in_specs=[whole] * 4 + [weight],
            out_specs=[out] + ([pl.BlockSpec((4, rows, tile), lambda i, td: (0, 0, i))] if mode == "a" else [out] * 3),
            scratch_shapes=[pltpu.VMEM((4 * rows, depth), BF16)],
        ),
        out_shape=[jax.ShapeDtypeStruct((rows, width), F32)]
        + ([jax.ShapeDtypeStruct((4, rows, width), BF16)] if mode == "a" else [jax.ShapeDtypeStruct((rows, width), BF16)] * 3),
        compiler_params=pltpu.CompilerParams(vmem_limit_bytes=(8 if RESIDENT else 40) << 20),
        cost_estimate=pl.CostEstimate(
            flops=COST2 * 1000,
            bytes_accessed=COST2 * 1000,
            transcendentals=0,
        ),
        name="down",
    )(td, h0, h1, h2, h3, down_weight)


def per_device(tokens, gate_weight, up_weight, down_weight, block_ids, block_counts):
    d, t = lax.axis_index("dp"), lax.axis_index("tensor")
    td = (d ^ t).reshape(1).astype(jnp.int32)
    dt = jnp.stack([d ^ t, t]).astype(jnp.int32)
    dd = d.reshape(1).astype(jnp.int32)
    active = active_units(block_ids, block_counts, gate_weight.shape[1])
    turn = [(a * 4 + b, b * 4 + a) for a in range(4) for b in range(4)]
    starts = [sum(SIZES[:c]) for c in range(CHUNKS + 1)]
    swap = lambda x, axis, mask: lax.ppermute(x, axis, xor_perm(4, mask))
    after = lambda x, *earlier: lax.optimization_barrier((x, *earlier))[0]
    blocks, mine, keep, send, near, across, hidden, far, pair = ([None] * CHUNKS for _ in range(9))
    parts, got, outs = {}, {}, {}
    tick = [td]


    def turn_in(c):
        x = tokens[starts[c] : starts[c + 1]]
        if c > 0:
            x = after(x, mine[c - 1])
        mine[c] = lax.ppermute(x, ("dp", "tensor"), turn)

    def spread(c):
        x = mine[c]
        if c > 0 and AFTER:
            x = after(x, *blocks[c - 1])
        if SPREAD == "a":
            y = lax.all_to_all(jnp.broadcast_to(x, (4, *x.shape)), "tensor", 0, 0, tiled=True)
            blocks[c] = [y]
        else:
            one, two = swap(x, "tensor", 1), swap(x, "tensor", 2)
            three = swap(two, "tensor", 1) if CUBE[c] else swap(x, "tensor", 3)
            blocks[c] = [mine[c], one, two, three]

    def first(c):
        if c + 1 < CHUNKS:
            tick.append(mine[c + 1])
        keep[c], send[c] = gate_up(after(dd if SPREAD == "a" else td, *tick), blocks[c], gate_weight, up_weight)
        tick[:] = [send[c]]

    def near_sum(c):
        held = after(send[c], *blocks[c + 1][:3 if CUBE[c + 1] else 4]) if HOLD and c + 1 < CHUNKS else send[c]
        near[c] = swap(held, "dp", 1)

    def add(c):
        x, _ = lax.optimization_barrier((keep[c], tuple(tick)))
        keep[c] = x
        side = near[c][1]
        if HOLD2 and c == 0:
            side = after(side, blocks[1][3])
        summed = (x[1] + side.astype(F32)).astype(BF16)
        across[c] = swap(summed, "dp", 2)
        tick[:] = [summed]

    def gated(c):
        x, _ = lax.optimization_barrier((keep[c], tuple(tick)))
        total = x[0] + near[c][0].astype(F32) + across[c].astype(F32)
        hidden[c] = (jnp.maximum(total[0], 0.0) * total[1] * active).astype(BF16)
        far[c] = swap(hidden[c], "dp", 2)
        pair[c] = [swap(hidden[c], "dp", 1), swap(far[c], "dp", 1)]
        tick[:] = [hidden[c]]

    def second(c, h):
        parts[c, h] = down(after(dt, *tick), hidden[c], pair[c][0], far[c], pair[c][1], down_weight, h, HALVES[c], MODE[c])
        if MODE[c] == "a":
            got[c, h] = lax.all_to_all(parts[c, h][1], "tensor", 0, 0, tiled=True)
        else:
            got[c, h] = [swap(parts[c, h][j], "tensor", j) for j in (1, 2, 3)]
        tick[:] = [parts[c, h][1]]

    def mix(c, h):
        mixed, _ = lax.optimization_barrier((parts[c, h][0], tuple(tick)))
        for j in range(len(got[c, h]) if MODE[c] == "x" else 4):
            g = got[c, h][j].astype(F32)
            mixed = mixed + (g if MODE[c] == "x" else jnp.where(t == j, 0.0, g))
        mixed = mixed.astype(BF16)
        outs[c, h] = lax.ppermute(mixed, ("dp", "tensor"), turn)
        tick[:] = [mixed]

    turn_in(0)
    spread(0)
    turn_in(1)
    first(0)
    spread(1)
    near_sum(0)
    add(0)
    first(1)
    near_sum(1)
    gated(0)
    add(1)
    for h in range(HALVES[0]):
        second(0, h)
    gated(1)
    second(1, 0)
    if MIXAT == 0:
        for h in range(HALVES[0]):
            mix(0, h)
    for h in range(1, HALVES[1]):
        second(1, h)
    if MIXAT == 1:
        for h in range(HALVES[0]):
            mix(0, h)
    for h in range(HALVES[1]):
        mix(1, h)
    return jnp.concatenate(
        [jnp.concatenate([outs[c, h] for h in range(HALVES[c])], axis=1) for c in range(CHUNKS)], axis=0
    )


def per_device_general(tokens, gate_weight, up_weight, down_weight, block_ids, block_counts):
    gathered = lax.all_gather(tokens, "tensor", axis=1, tiled=True)
    turned = lax.all_to_all(gathered, "dp", 1, 0, tiled=True)
    active = active_units(block_ids, block_counts, gate_weight.shape[1])
    sums = [
        lax.psum_scatter(
            jnp.dot(turned, w, preferred_element_type=F32), "dp", scatter_dimension=0, tiled=True
        )
        for w in (gate_weight, up_weight)
    ]
    hidden = (jnp.maximum(sums[0], 0.0) * sums[1] * active).astype(BF16)
    hidden = lax.all_gather(hidden, "dp", axis=0, tiled=True)
    partial = jnp.dot(hidden, down_weight, preferred_element_type=F32)
    partial = lax.all_to_all(partial, "dp", 0, 1, tiled=True)
    return lax.psum_scatter(partial, "tensor", scatter_dimension=1, tiled=True).astype(BF16)


def solution(mesh):
    placed = (
        P(("groups", "dp"), "tensor"),
        P("dp", "tensor"),
        P("dp", "tensor"),
        P("tensor", "dp"),
        P(("groups", "tensor")),
        P(("groups", "tensor")),
    )
    square = mesh.shape["dp"] == 4 and mesh.shape["tensor"] == 4
    return jax.shard_map(
        per_device if square else per_device_general,
        mesh=mesh,
        in_specs=placed,
        out_specs=P(("groups", "dp"), "tensor"),
        check_vma=False,
    )
```

```python
import jax
import jax.numpy as jnp
from jax import lax
from jax.experimental import pallas as pl
from jax.experimental.pallas import tpu as pltpu
from jax.sharding import PartitionSpec as P

BF16, F32 = jnp.bfloat16, jnp.float32


def xor_perm(size, mask):
    return [(i, i ^ mask) for i in range(size)]


def active_units(block_ids, block_counts, unit_count):
    block_total = block_ids.shape[0]
    places = jnp.arange(block_total, dtype=jnp.int32)
    match = (block_ids[:, None] % block_total == places[None, :]) & (
        places < block_counts[0]
    )[:, None]
    active = jnp.any(match, axis=0).astype(F32)
    return jnp.repeat(active, unit_count // block_total)


def gate_up_kernel(td_ref, *refs):
    blocks, (gate_ref, up_ref, keep_ref, near_ref, far_ref, xs) = refs[:4], refs[4:]
    rows = xs.shape[0] // 4

    @pl.when(pl.program_id(0) == 0)
    def _():
        for j in range(4):
            place = pl.multiple_of((j ^ td_ref[0]) * rows, rows)
            xs[pl.ds(place, rows), :] = blocks[j][...]

    for i, w in enumerate((gate_ref, up_ref)):
        acc = jnp.dot(xs[...], w[...], preferred_element_type=F32)
        keep_ref[0, i] = acc[:rows]
        near_ref[i] = acc[rows : 2 * rows].astype(BF16)
        keep_ref[1, i] = acc[2 * rows : 3 * rows]
        far_ref[i] = acc[3 * rows :].astype(BF16)


def gate_up(td, blocks, gate_weight, up_weight, tile=1024):
    rows, depth = blocks[0].shape
    units = gate_weight.shape[1]
    whole = pl.BlockSpec((rows, depth), lambda i, td: (0, 0))
    weight = pl.BlockSpec((depth, tile), lambda i, td: (0, i))
    out = pl.BlockSpec((2, 2, rows, tile), lambda i, td: (0, 0, 0, i))
    side = pl.BlockSpec((2, rows, tile), lambda i, td: (0, 0, i))
    return pl.pallas_call(
        gate_up_kernel,
        grid_spec=pltpu.PrefetchScalarGridSpec(
            num_scalar_prefetch=1,
            grid=(units // tile,),
            in_specs=[whole] * 4 + [weight] * 2,
            out_specs=[out, side, side],
            scratch_shapes=[pltpu.VMEM((4 * rows, depth), BF16)],
        ),
        out_shape=[
            jax.ShapeDtypeStruct((2, 2, rows, units), F32),
            jax.ShapeDtypeStruct((2, rows, units), BF16),
            jax.ShapeDtypeStruct((2, rows, units), BF16),
        ],
        compiler_params=pltpu.CompilerParams(vmem_limit_bytes=40 << 20),
        cost_estimate=pl.CostEstimate(flops=20_000_000, bytes_accessed=20_000_000, transcendentals=0),
        name="gate_up",
    )(td, *blocks, gate_weight, up_weight)


def down_kernel(td_ref, h0, h1, h2, h3, down_ref, own_ref, *refs):
    outs, hs = refs[:-1], refs[-1]
    rows = h0.shape[0]

    @pl.when(pl.program_id(0) == 0)
    def _():
        for k, h in enumerate((h0, h1, h2, h3)):
            place = pl.multiple_of((k ^ td_ref[0]) * rows, rows)
            hs[pl.ds(place, rows), :] = h[...]

    acc = jnp.dot(hs[...], down_ref[...], preferred_element_type=F32)
    own_ref[...] = acc[:rows]
    if len(outs) == 1:
        for j in range(4):
            outs[0][j ^ td_ref[1]] = acc[j * rows : (j + 1) * rows].astype(BF16)
    else:
        for j in (1, 2, 3):
            outs[j - 1][...] = acc[j * rows : (j + 1) * rows].astype(BF16)


def down(td, hidden, down_weight, part, parts, stacked, tile=512):
    rows, depth = hidden[0].shape
    width = down_weight.shape[1] // parts
    first = part * (width // tile)
    whole = pl.BlockSpec((rows, depth), lambda i, td: (0, 0))
    weight = pl.BlockSpec((depth, tile), lambda i, td: (0, first + i))
    out = pl.BlockSpec((rows, tile), lambda i, td: (0, i))
    stack = pl.BlockSpec((4, rows, tile), lambda i, td: (0, 0, i))
    sent = [(4, rows, width)] if stacked else [(rows, width)] * 3
    return pl.pallas_call(
        down_kernel,
        grid_spec=pltpu.PrefetchScalarGridSpec(
            num_scalar_prefetch=1,
            grid=(width // tile,),
            in_specs=[whole] * 4 + [weight],
            out_specs=[out] + ([stack] if stacked else [out] * 3),
            scratch_shapes=[pltpu.VMEM((4 * rows, depth), BF16)],
        ),
        out_shape=[jax.ShapeDtypeStruct((rows, width), F32)]
        + [jax.ShapeDtypeStruct(shape, BF16) for shape in sent],
        compiler_params=pltpu.CompilerParams(vmem_limit_bytes=40 << 20),
        cost_estimate=pl.CostEstimate(flops=1_000_000, bytes_accessed=1_000_000, transcendentals=0),
        name="down",
    )(td, *hidden, down_weight)


def per_device(tokens, gate_weight, up_weight, down_weight, block_ids, block_counts):
    d, t = lax.axis_index("dp"), lax.axis_index("tensor")
    td = (d ^ t).reshape(1).astype(jnp.int32)
    dt = jnp.stack([d ^ t, t]).astype(jnp.int32)
    active = active_units(block_ids, block_counts, gate_weight.shape[1])
    turn = [(a * 4 + b, b * 4 + a) for a in range(4) for b in range(4)]
    rows = tokens.shape[0] // 2
    swap = lambda x, axis, mask: lax.ppermute(x, axis, xor_perm(4, mask))
    after = lambda x, *earlier: lax.optimization_barrier((x, *earlier))[0]
    mine, blocks, keep, send, near, across, hidden, partial, got, outs = ({} for _ in range(10))
    tick = [td]

    def turn_in(c):
        x = tokens[c * rows : (c + 1) * rows]
        mine[c] = lax.ppermute(x if c == 0 else after(x, mine[c - 1]), ("dp", "tensor"), turn)

    def spread(c):
        x = mine[c] if c == 0 else after(mine[c], *blocks[c - 1])
        one, two = swap(x, "tensor", 1), swap(x, "tensor", 2)
        blocks[c] = [mine[c], one, two, swap(two, "tensor", 1)]

    def first(c):
        keep[c], *send[c] = gate_up(after(td, *tick), blocks[c], gate_weight, up_weight)
        tick[:] = send[c]

    def to_core(c, *earlier):
        held = lax.optimization_barrier((*send[c], *earlier))[:2] if earlier else send[c]
        near[c] = [swap(x, "dp", 1) for x in held]

    def to_chip(c):
        keep[c] = lax.optimization_barrier((keep[c], *tick))[0]
        summed = (keep[c][1] + near[c][1].astype(F32)).astype(BF16)
        across[c] = swap(summed, "dp", 2)
        tick[:] = [summed]

    def gated(c):
        x = after(keep[c], *tick)
        total = x[0] + near[c][0].astype(F32) + across[c].astype(F32)
        own = (jnp.maximum(total[0], 0.0) * total[1] * active).astype(BF16)
        far = swap(own, "dp", 2)
        hidden[c] = [own, swap(own, "dp", 1), far, swap(far, "dp", 1)]
        tick[:] = [own]

    def second(c, h, parts):
        stacked = parts == 1
        partial[c, h], *sent = down(after(dt, *tick), hidden[c], down_weight, h, parts, stacked)
        if stacked:
            arrived = lax.all_to_all(sent[0], "tensor", 0, 0, tiled=True)
            got[c, h] = [(arrived[j], t == j) for j in range(4)]
        else:
            got[c, h] = [(swap(sent[j - 1], "tensor", j), None) for j in (1, 2, 3)]
        tick[:] = [sent[0]]

    def mix(c, h):
        mixed = after(partial[c, h], *tick)
        for x, is_own in got[c, h]:
            x = x.astype(F32)
            mixed = mixed + (x if is_own is None else jnp.where(is_own, 0.0, x))
        mixed = mixed.astype(BF16)
        outs[c, h] = lax.ppermute(mixed, ("dp", "tensor"), turn)
        tick[:] = [mixed]

    turn_in(0)
    spread(0)
    turn_in(1)
    tick.append(mine[1])
    first(0)
    spread(1)
    to_core(0, *blocks[1][:3])
    to_chip(0)
    first(1)
    to_core(1)
    gated(0)
    to_chip(1)
    second(0, 0, 1)
    gated(1)
    second(1, 0, 2)
    mix(0, 0)
    second(1, 1, 2)
    mix(1, 0)
    mix(1, 1)
    last = jnp.concatenate([outs[1, 0], outs[1, 1]], axis=1)
    return jnp.concatenate([outs[0, 0], last], axis=0)


def per_device_general(tokens, gate_weight, up_weight, down_weight, block_ids, block_counts):
    gathered = lax.all_gather(tokens, "tensor", axis=1, tiled=True)
    turned = lax.all_to_all(gathered, "dp", 1, 0, tiled=True)
    active = active_units(block_ids, block_counts, gate_weight.shape[1])
    sums = [
        lax.psum_scatter(
            jnp.dot(turned, w, preferred_element_type=F32), "dp", scatter_dimension=0, tiled=True
        )
        for w in (gate_weight, up_weight)
    ]
    hidden = (jnp.maximum(sums[0], 0.0) * sums[1] * active).astype(BF16)
    hidden = lax.all_gather(hidden, "dp", axis=0, tiled=True)
    partial = jnp.dot(hidden, down_weight, preferred_element_type=F32)
    partial = lax.all_to_all(partial, "dp", 0, 1, tiled=True)
    return lax.psum_scatter(partial, "tensor", scatter_dimension=1, tiled=True).astype(BF16)


def solution(mesh):
    placed = (
        P(("groups", "dp"), "tensor"),
        P("dp", "tensor"),
        P("dp", "tensor"),
        P("tensor", "dp"),
        P(("groups", "tensor")),
        P(("groups", "tensor")),
    )
    square = mesh.shape["dp"] == 4 and mesh.shape["tensor"] == 4
    return jax.shard_map(
        per_device if square else per_device_general,
        mesh=mesh,
        in_specs=placed,
        out_specs=P(("groups", "dp"), "tensor"),
        check_vma=False,
    )
```

```python
import jax
import jax.numpy as jnp
from jax import lax
from jax.experimental import pallas as pl
from jax.experimental.pallas import tpu as pltpu
from jax.sharding import PartitionSpec as P

BF16, F32 = jnp.bfloat16, jnp.float32


def xor_perm(size, mask):
    return [(i, i ^ mask) for i in range(size)]


def active_units(block_ids, block_counts, unit_count):
    block_total = block_ids.shape[0]
    places = jnp.arange(block_total, dtype=jnp.int32)
    match = (block_ids[:, None] % block_total == places[None, :]) & (
        places < block_counts[0]
    )[:, None]
    active = jnp.any(match, axis=0).astype(F32)
    return jnp.repeat(active, unit_count // block_total)


def gate_up_kernel(td_ref, *refs):
    blocks, (gate_ref, up_ref, keep_ref, near_ref, far_ref, xs) = refs[:4], refs[4:]
    rows = xs.shape[0] // 4

    @pl.when(pl.program_id(0) == 0)
    def _():
        for j in range(4):
            place = pl.multiple_of((j ^ td_ref[0]) * rows, rows)
            xs[pl.ds(place, rows), :] = blocks[j][...]

    for i, w in enumerate((gate_ref, up_ref)):
        acc = jnp.dot(xs[...], w[...], preferred_element_type=F32)
        keep_ref[0, i] = acc[:rows]
        near_ref[i] = acc[rows : 2 * rows].astype(BF16)
        keep_ref[1, i] = acc[2 * rows : 3 * rows]
        far_ref[i] = acc[3 * rows :].astype(BF16)


def gate_up(td, blocks, gate_weight, up_weight, tile=1024):
    rows, depth = blocks[0].shape
    units = gate_weight.shape[1]
    whole = pl.BlockSpec((rows, depth), lambda i, td: (0, 0))
    weight = pl.BlockSpec((depth, tile), lambda i, td: (0, i))
    out = pl.BlockSpec((2, 2, rows, tile), lambda i, td: (0, 0, 0, i))
    side = pl.BlockSpec((2, rows, tile), lambda i, td: (0, 0, i))
    return pl.pallas_call(
        gate_up_kernel,
        grid_spec=pltpu.PrefetchScalarGridSpec(
            num_scalar_prefetch=1,
            grid=(units // tile,),
            in_specs=[whole] * 4 + [weight] * 2,
            out_specs=[out, side, side],
            scratch_shapes=[pltpu.VMEM((4 * rows, depth), BF16)],
        ),
        out_shape=[
            jax.ShapeDtypeStruct((2, 2, rows, units), F32),
            jax.ShapeDtypeStruct((2, rows, units), BF16),
            jax.ShapeDtypeStruct((2, rows, units), BF16),
        ],
        compiler_params=pltpu.CompilerParams(vmem_limit_bytes=40 << 20),
        cost_estimate=pl.CostEstimate(flops=20_000_000, bytes_accessed=20_000_000, transcendentals=0),
        name="gate_up",
    )(td, *blocks, gate_weight, up_weight)


def down_kernel(td_ref, h0, h1, h2, h3, down_ref, own_ref, *refs):
    outs, hs = refs[:-1], refs[-1]
    rows = h0.shape[0]

    @pl.when(pl.program_id(0) == 0)
    def _():
        for k, h in enumerate((h0, h1, h2, h3)):
            place = pl.multiple_of((k ^ td_ref[0]) * rows, rows)
            hs[pl.ds(place, rows), :] = h[...]

    acc = jnp.dot(hs[...], down_ref[...], preferred_element_type=F32)
    own_ref[...] = acc[:rows]
    if len(outs) == 1:
        for j in range(4):
            outs[0][j ^ td_ref[1]] = acc[j * rows : (j + 1) * rows].astype(BF16)
    else:
        for j in (1, 2, 3):
            outs[j - 1][...] = acc[j * rows : (j + 1) * rows].astype(outs[j - 1].dtype)


def down(td, hidden, down_weight, part, parts, stacked, tile=512):
    rows, depth = hidden[0].shape
    width = down_weight.shape[1] // parts
    first = part * (width // tile)
    whole = pl.BlockSpec((rows, depth), lambda i, td: (0, 0))
    weight = pl.BlockSpec((depth, tile), lambda i, td: (0, first + i))
    out = pl.BlockSpec((rows, tile), lambda i, td: (0, i))
    stack = pl.BlockSpec((4, rows, tile), lambda i, td: (0, 0, i))
    sent = [((4, rows, width), BF16)] if stacked else [((rows, width), t) for t in (BF16, F32, BF16)]
    return pl.pallas_call(
        down_kernel,
        grid_spec=pltpu.PrefetchScalarGridSpec(
            num_scalar_prefetch=1,
            grid=(width // tile,),
            in_specs=[whole] * 4 + [weight],
            out_specs=[out] + ([stack] if stacked else [out] * 3),
            scratch_shapes=[pltpu.VMEM((4 * rows, depth), BF16)],
        ),
        out_shape=[jax.ShapeDtypeStruct((rows, width), F32)]
        + [jax.ShapeDtypeStruct(*each) for each in sent],
        compiler_params=pltpu.CompilerParams(vmem_limit_bytes=40 << 20),
        cost_estimate=pl.CostEstimate(flops=1_000_000, bytes_accessed=1_000_000, transcendentals=0),
        name="down",
    )(td, *hidden, down_weight)


def per_device(tokens, gate_weight, up_weight, down_weight, block_ids, block_counts):
    d, t = lax.axis_index("dp"), lax.axis_index("tensor")
    td = (d ^ t).reshape(1).astype(jnp.int32)
    dt = jnp.stack([d ^ t, t]).astype(jnp.int32)
    active = active_units(block_ids, block_counts, gate_weight.shape[1])
    turn = [(a * 4 + b, b * 4 + a) for a in range(4) for b in range(4)]
    rows = tokens.shape[0] // 2
    swap = lambda x, axis, mask: lax.ppermute(x, axis, xor_perm(4, mask))
    after = lambda x, *earlier: lax.optimization_barrier((x, *earlier))[0]
    mine, blocks, keep, send, near, across, hidden, partial, got, outs = ({} for _ in range(10))
    kept, passed = {}, {}
    tick = [td]

    def turn_in(c):
        x = tokens[c * rows : (c + 1) * rows]
        mine[c] = lax.ppermute(x if c == 0 else after(x, mine[c - 1]), ("dp", "tensor"), turn)

    def spread(c):
        x = mine[c] if c == 0 else after(mine[c], *blocks[c - 1])
        one, two = swap(x, "tensor", 1), swap(x, "tensor", 2)
        blocks[c] = [mine[c], one, two, swap(two, "tensor", 1)]

    def first(c):
        keep[c], *send[c] = gate_up(after(td, *tick), blocks[c], gate_weight, up_weight)
        tick[:] = send[c]

    def to_core(c, *earlier):
        held = lax.optimization_barrier((*send[c], *earlier))[:2] if earlier else send[c]
        near[c] = [swap(x, "dp", 1) for x in held]

    def to_chip(c):
        keep[c] = lax.optimization_barrier((keep[c], *tick))[0]
        summed = (keep[c][1] + near[c][1].astype(F32)).astype(BF16)
        across[c] = swap(summed, "dp", 2)
        tick[:] = [summed]

    def gated(c):
        x = after(keep[c], *tick)
        total = x[0] + near[c][0].astype(F32) + across[c].astype(F32)
        own = (jnp.maximum(total[0], 0.0) * total[1] * active).astype(BF16)
        far = swap(own, "dp", 2)
        hidden[c] = [own, swap(own, "dp", 1), far, swap(far, "dp", 1)]
        tick[:] = [own]

    def second(c, h, parts):
        stacked = parts == 1
        partial[c, h], *sent = down(after(dt, *tick), hidden[c], down_weight, h, parts, stacked)
        if stacked:
            arrived = lax.all_to_all(sent[0], "tensor", 0, 0, tiled=True)
            got[c, h] = [(arrived[j], t == j) for j in range(4)]
        else:
            kept[h] = sent[1]
            got[c, h] = [(swap(sent[0], "tensor", 1), None)]
            passed[h] = swap(sent[2], "tensor", 1)
        tick[:] = [sent[0]]

    def pass_on(c, h):
        summed = (after(kept[h], *tick) + passed[h].astype(F32)).astype(BF16)
        got[c, h].append((swap(summed, "tensor", 2), None))
        tick[:] = [summed]

    def mix(c, h):
        mixed = after(partial[c, h], *tick)
        for x, is_own in got[c, h]:
            x = x.astype(F32)
            mixed = mixed + (x if is_own is None else jnp.where(is_own, 0.0, x))
        mixed = mixed.astype(BF16)
        outs[c, h] = lax.ppermute(mixed, ("dp", "tensor"), turn)
        tick[:] = [mixed]

    turn_in(0)
    spread(0)
    turn_in(1)
    tick.append(mine[1])
    first(0)
    spread(1)
    to_core(0, *blocks[1][:3])
    to_chip(0)
    first(1)
    to_core(1)
    gated(0)
    to_chip(1)
    second(0, 0, 1)
    gated(1)
    second(1, 0, 2)
    mix(0, 0)
    second(1, 1, 2)
    pass_on(1, 0)
    pass_on(1, 1)
    mix(1, 0)
    mix(1, 1)
    last = jnp.concatenate([outs[1, 0], outs[1, 1]], axis=1)
    return jnp.concatenate([outs[0, 0], last], axis=0)


def per_device_general(tokens, gate_weight, up_weight, down_weight, block_ids, block_counts):
    gathered = lax.all_gather(tokens, "tensor", axis=1, tiled=True)
    turned = lax.all_to_all(gathered, "dp", 1, 0, tiled=True)
    active = active_units(block_ids, block_counts, gate_weight.shape[1])
    sums = [
        lax.psum_scatter(
            jnp.dot(turned, w, preferred_element_type=F32), "dp", scatter_dimension=0, tiled=True
        )
        for w in (gate_weight, up_weight)
    ]
    hidden = (jnp.maximum(sums[0], 0.0) * sums[1] * active).astype(BF16)
    hidden = lax.all_gather(hidden, "dp", axis=0, tiled=True)
    partial = jnp.dot(hidden, down_weight, preferred_element_type=F32)
    partial = lax.all_to_all(partial, "dp", 0, 1, tiled=True)
    return lax.psum_scatter(partial, "tensor", scatter_dimension=1, tiled=True).astype(BF16)


def solution(mesh):
    placed = (
        P(("groups", "dp"), "tensor"),
        P("dp", "tensor"),
        P("dp", "tensor"),
        P("tensor", "dp"),
        P(("groups", "tensor")),
        P(("groups", "tensor")),
    )
    square = mesh.shape["dp"] == 4 and mesh.shape["tensor"] == 4
    return jax.shard_map(
        per_device if square else per_device_general,
        mesh=mesh,
        in_specs=placed,
        out_specs=P(("groups", "dp"), "tensor"),
        check_vma=False,
    )
```

```python
import jax
import jax.numpy as jnp
from jax import lax
from jax.experimental import pallas as pl
from jax.experimental.pallas import tpu as pltpu
from jax.sharding import PartitionSpec as P

BF16, F32 = jnp.bfloat16, jnp.float32


def xor_perm(size, mask):
    return [(i, i ^ mask) for i in range(size)]


def active_units(block_ids, block_counts, unit_count):
    block_total = block_ids.shape[0]
    places = jnp.arange(block_total, dtype=jnp.int32)
    match = (block_ids[:, None] % block_total == places[None, :]) & (
        places < block_counts[0]
    )[:, None]
    active = jnp.any(match, axis=0).astype(F32)
    return jnp.repeat(active, unit_count // block_total)


def gate_up_kernel(td_ref, *refs):
    blocks, (gate_ref, up_ref, keep_ref, near_ref, far_ref, xs) = refs[:4], refs[4:]
    rows = xs.shape[0] // 4

    @pl.when(pl.program_id(0) == 0)
    def _():
        for j in range(4):
            place = pl.multiple_of((j ^ td_ref[0]) * rows, rows)
            xs[pl.ds(place, rows), :] = blocks[j][...]

    for i, w in enumerate((gate_ref, up_ref)):
        acc = jnp.dot(xs[...], w[...], preferred_element_type=F32)
        keep_ref[0, i] = acc[:rows]
        near_ref[i] = acc[rows : 2 * rows].astype(BF16)
        keep_ref[1, i] = acc[2 * rows : 3 * rows]
        far_ref[i] = acc[3 * rows :].astype(BF16)


def gate_up(td, blocks, gate_weight, up_weight, tile=1024):
    rows, depth = blocks[0].shape
    units = gate_weight.shape[1]
    whole = pl.BlockSpec((rows, depth), lambda i, td: (0, 0))
    weight = pl.BlockSpec((depth, tile), lambda i, td: (0, i))
    out = pl.BlockSpec((2, 2, rows, tile), lambda i, td: (0, 0, 0, i))
    side = pl.BlockSpec((2, rows, tile), lambda i, td: (0, 0, i))
    return pl.pallas_call(
        gate_up_kernel,
        grid_spec=pltpu.PrefetchScalarGridSpec(
            num_scalar_prefetch=1,
            grid=(units // tile,),
            in_specs=[whole] * 4 + [weight] * 2,
            out_specs=[out, side, side],
            scratch_shapes=[pltpu.VMEM((4 * rows, depth), BF16)],
        ),
        out_shape=[
            jax.ShapeDtypeStruct((2, 2, rows, units), F32),
            jax.ShapeDtypeStruct((2, rows, units), BF16),
            jax.ShapeDtypeStruct((2, rows, units), BF16),
        ],
        compiler_params=pltpu.CompilerParams(vmem_limit_bytes=40 << 20),
        cost_estimate=pl.CostEstimate(flops=20_000_000, bytes_accessed=20_000_000, transcendentals=0),
        name="gate_up",
    )(td, *blocks, gate_weight, up_weight)


def down_kernel(td_ref, h0, h1, h2, h3, down_ref, own_ref, *refs):
    outs, hs = refs[:-1], refs[-1]
    rows = h0.shape[0]

    @pl.when(pl.program_id(0) == 0)
    def _():
        for k, h in enumerate((h0, h1, h2, h3)):
            place = pl.multiple_of((k ^ td_ref[0]) * rows, rows)
            hs[pl.ds(place, rows), :] = h[...]

    acc = jnp.dot(hs[...], down_ref[...], preferred_element_type=F32)
    own_ref[...] = acc[:rows]
    if len(outs) == 1:
        for j in range(4):
            outs[0][j ^ td_ref[1]] = acc[j * rows : (j + 1) * rows].astype(BF16)
    else:
        for j in (1, 2, 3):
            outs[j - 1][...] = acc[j * rows : (j + 1) * rows].astype(outs[j - 1].dtype)


def down(td, hidden, down_weight, part, parts, stacked, tile=512):
    rows, depth = hidden[0].shape
    width = down_weight.shape[1] // parts
    first = part * (width // tile)
    whole = pl.BlockSpec((rows, depth), lambda i, td: (0, 0))
    weight = pl.BlockSpec((depth, tile), lambda i, td: (0, first + i))
    out = pl.BlockSpec((rows, tile), lambda i, td: (0, i))
    stack = pl.BlockSpec((4, rows, tile), lambda i, td: (0, 0, i))
    sent = [((4, rows, width), BF16)] if stacked else [((rows, width), t) for t in (BF16, F32, BF16)]
    return pl.pallas_call(
        down_kernel,
        grid_spec=pltpu.PrefetchScalarGridSpec(
            num_scalar_prefetch=1,
            grid=(width // tile,),
            in_specs=[whole] * 4 + [weight],
            out_specs=[out] + ([stack] if stacked else [out] * 3),
            scratch_shapes=[pltpu.VMEM((4 * rows, depth), BF16)],
        ),
        out_shape=[jax.ShapeDtypeStruct((rows, width), F32)]
        + [jax.ShapeDtypeStruct(*each) for each in sent],
        compiler_params=pltpu.CompilerParams(vmem_limit_bytes=40 << 20),
        cost_estimate=pl.CostEstimate(flops=1_000_000, bytes_accessed=1_000_000, transcendentals=0),
        name="down",
    )(td, *hidden, down_weight)


def per_device(tokens, gate_weight, up_weight, down_weight, block_ids, block_counts):
    d, t = lax.axis_index("dp"), lax.axis_index("tensor")
    td = (d ^ t).reshape(1).astype(jnp.int32)
    dt = jnp.stack([d ^ t, t]).astype(jnp.int32)
    active = active_units(block_ids, block_counts, gate_weight.shape[1])
    turn = [(a * 4 + b, b * 4 + a) for a in range(4) for b in range(4)]
    rows = tokens.shape[0] // 2
    swap = lambda x, axis, mask: lax.ppermute(x, axis, xor_perm(4, mask))
    after = lambda x, *earlier: lax.optimization_barrier((x, *earlier))[0]
    mine, blocks, keep, send, near, across, hidden, partial, got, outs = ({} for _ in range(10))
    kept, passed = {}, {}
    tick = [td]

    def turn_in(c):
        x = tokens[c * rows : (c + 1) * rows]
        mine[c] = lax.ppermute(x if c == 0 else after(x, mine[c - 1]), ("dp", "tensor"), turn)

    def spread(c):
        x = mine[c] if c == 0 else after(mine[c], *blocks[c - 1])
        one, two = swap(x, "tensor", 1), swap(x, "tensor", 2)
        blocks[c] = [mine[c], one, two, swap(two, "tensor", 1)]

    def first(c):
        keep[c], *send[c] = gate_up(after(td, *tick), blocks[c], gate_weight, up_weight)
        tick[:] = send[c]

    def to_core(c, *earlier):
        held = lax.optimization_barrier((*send[c], *earlier))[:2] if earlier else send[c]
        near[c] = [swap(x, "dp", 1) for x in held]

    def to_chip(c):
        keep[c] = lax.optimization_barrier((keep[c], *tick))[0]
        summed = (keep[c][1] + near[c][1].astype(F32)).astype(BF16)
        across[c] = swap(summed, "dp", 2)
        tick[:] = [summed]

    def gated(c):
        x = after(keep[c], *tick)
        total = x[0] + near[c][0].astype(F32) + across[c].astype(F32)
        own = (jnp.maximum(total[0], 0.0) * total[1] * active).astype(BF16)
        far = swap(own, "dp", 2)
        hidden[c] = [own, swap(own, "dp", 1), far, swap(far, "dp", 1)]
        tick[:] = [own]

    def second(c, h, parts):
        stacked = parts == 1
        partial[c, h], *sent = down(after(dt, *tick), hidden[c], down_weight, h, parts, stacked)
        if stacked:
            arrived = lax.all_to_all(sent[0], "tensor", 0, 0, tiled=True)
            got[c, h] = [(arrived[j], t == j) for j in range(4)]
        else:
            kept[h] = sent[1]
            passed[h] = swap(sent[2], "tensor", 1)
            direct = after(sent[0], passed[h]) if h else sent[0]
            got[c, h] = [(swap(direct, "tensor", 1), None)]
        tick[:] = [sent[0]]

    def pass_on(c, h):
        summed = (after(kept[h], *tick) + passed[h].astype(F32)).astype(BF16)
        got[c, h].append((swap(summed, "tensor", 2), None))
        tick[:] = [summed]

    def mix(c, h):
        mixed = after(partial[c, h], *tick)
        for x, is_own in got[c, h]:
            x = x.astype(F32)
            mixed = mixed + (x if is_own is None else jnp.where(is_own, 0.0, x))
        mixed = mixed.astype(BF16)
        outs[c, h] = lax.ppermute(mixed, ("dp", "tensor"), turn)
        tick[:] = [mixed]

    turn_in(0)
    spread(0)
    turn_in(1)
    tick.append(mine[1])
    first(0)
    spread(1)
    to_core(0, *blocks[1][:3])
    to_chip(0)
    first(1)
    to_core(1)
    gated(0)
    to_chip(1)
    second(0, 0, 1)
    gated(1)
    second(1, 0, 2)
    mix(0, 0)
    second(1, 1, 2)
    pass_on(1, 0)
    pass_on(1, 1)
    mix(1, 0)
    mix(1, 1)
    last = jnp.concatenate([outs[1, 0], outs[1, 1]], axis=1)
    return jnp.concatenate([outs[0, 0], last], axis=0)


def per_device_general(tokens, gate_weight, up_weight, down_weight, block_ids, block_counts):
    gathered = lax.all_gather(tokens, "tensor", axis=1, tiled=True)
    turned = lax.all_to_all(gathered, "dp", 1, 0, tiled=True)
    active = active_units(block_ids, block_counts, gate_weight.shape[1])
    sums = [
        lax.psum_scatter(
            jnp.dot(turned, w, preferred_element_type=F32), "dp", scatter_dimension=0, tiled=True
        )
        for w in (gate_weight, up_weight)
    ]
    hidden = (jnp.maximum(sums[0], 0.0) * sums[1] * active).astype(BF16)
    hidden = lax.all_gather(hidden, "dp", axis=0, tiled=True)
    partial = jnp.dot(hidden, down_weight, preferred_element_type=F32)
    partial = lax.all_to_all(partial, "dp", 0, 1, tiled=True)
    return lax.psum_scatter(partial, "tensor", scatter_dimension=1, tiled=True).astype(BF16)


def solution(mesh):
    placed = (
        P(("groups", "dp"), "tensor"),
        P("dp", "tensor"),
        P("dp", "tensor"),
        P("tensor", "dp"),
        P(("groups", "tensor")),
        P(("groups", "tensor")),
    )
    square = mesh.shape["dp"] == 4 and mesh.shape["tensor"] == 4
    return jax.shard_map(
        per_device if square else per_device_general,
        mesh=mesh,
        in_specs=placed,
        out_specs=P(("groups", "dp"), "tensor"),
        check_vma=False,
    )
```

```python
import jax
import jax.numpy as jnp
from jax import lax
from jax.experimental import pallas as pl
from jax.experimental.pallas import tpu as pltpu
from jax.sharding import PartitionSpec as P

BF16, F32 = jnp.bfloat16, jnp.float32


def xor_perm(size, mask):
    return [(i, i ^ mask) for i in range(size)]


def active_units(block_ids, block_counts, unit_count):
    block_total = block_ids.shape[0]
    places = jnp.arange(block_total, dtype=jnp.int32)
    match = (block_ids[:, None] % block_total == places[None, :]) & (
        places < block_counts[0]
    )[:, None]
    active = jnp.any(match, axis=0).astype(F32)
    return jnp.repeat(active, unit_count // block_total)


def gate_up_kernel(td_ref, *refs):
    blocks, (gate_ref, up_ref, keep_ref, near_ref, far_ref, xs) = refs[:4], refs[4:]
    rows = xs.shape[0] // 4

    @pl.when(pl.program_id(0) == 0)
    def _():
        for j in range(4):
            place = pl.multiple_of((j ^ td_ref[0]) * rows, rows)
            xs[pl.ds(place, rows), :] = blocks[j][...]

    for i, w in enumerate((gate_ref, up_ref)):
        acc = jnp.dot(xs[...], w[...], preferred_element_type=F32)
        keep_ref[0, i] = acc[:rows]
        near_ref[i] = acc[rows : 2 * rows].astype(BF16)
        keep_ref[1, i] = acc[2 * rows : 3 * rows]
        far_ref[i] = acc[3 * rows :].astype(BF16)


def gate_up(td, blocks, gate_weight, up_weight, tile=1024):
    rows, depth = blocks[0].shape
    units = gate_weight.shape[1]
    whole = pl.BlockSpec((rows, depth), lambda i, td: (0, 0))
    weight = pl.BlockSpec((depth, tile), lambda i, td: (0, i))
    out = pl.BlockSpec((2, 2, rows, tile), lambda i, td: (0, 0, 0, i))
    side = pl.BlockSpec((2, rows, tile), lambda i, td: (0, 0, i))
    return pl.pallas_call(
        gate_up_kernel,
        grid_spec=pltpu.PrefetchScalarGridSpec(
            num_scalar_prefetch=1,
            grid=(units // tile,),
            in_specs=[whole] * 4 + [weight] * 2,
            out_specs=[out, side, side],
            scratch_shapes=[pltpu.VMEM((4 * rows, depth), BF16)],
        ),
        out_shape=[
            jax.ShapeDtypeStruct((2, 2, rows, units), F32),
            jax.ShapeDtypeStruct((2, rows, units), BF16),
            jax.ShapeDtypeStruct((2, rows, units), BF16),
        ],
        compiler_params=pltpu.CompilerParams(vmem_limit_bytes=40 << 20),
        cost_estimate=pl.CostEstimate(flops=20_000_000, bytes_accessed=20_000_000, transcendentals=0),
        name="gate_up",
    )(td, *blocks, gate_weight, up_weight)


def down_kernel(td_ref, h0, h1, h2, h3, down_ref, own_ref, *refs):
    outs, hs = refs[:-1], refs[-1]
    rows = h0.shape[0]

    @pl.when(pl.program_id(0) == 0)
    def _():
        for k, h in enumerate((h0, h1, h2, h3)):
            place = pl.multiple_of((k ^ td_ref[0]) * rows, rows)
            hs[pl.ds(place, rows), :] = h[...]

    acc = jnp.dot(hs[...], down_ref[...], preferred_element_type=F32)
    own_ref[...] = acc[:rows]
    if len(outs) == 1:
        for j in range(4):
            outs[0][j ^ td_ref[1]] = acc[j * rows : (j + 1) * rows].astype(BF16)
    else:
        for j in (1, 2, 3):
            outs[j - 1][...] = acc[j * rows : (j + 1) * rows].astype(outs[j - 1].dtype)


def down(td, hidden, down_weight, part, parts, stacked, tile=512):
    rows, depth = hidden[0].shape
    width = down_weight.shape[1] // parts
    first = part * (width // tile)
    whole = pl.BlockSpec((rows, depth), lambda i, td: (0, 0))
    weight = pl.BlockSpec((depth, tile), lambda i, td: (0, first + i))
    out = pl.BlockSpec((rows, tile), lambda i, td: (0, i))
    stack = pl.BlockSpec((4, rows, tile), lambda i, td: (0, 0, i))
    sent = [((4, rows, width), BF16)] if stacked else [((rows, width), t) for t in (BF16, F32, BF16)]
    return pl.pallas_call(
        down_kernel,
        grid_spec=pltpu.PrefetchScalarGridSpec(
            num_scalar_prefetch=1,
            grid=(width // tile,),
            in_specs=[whole] * 4 + [weight],
            out_specs=[out] + ([stack] if stacked else [out] * 3),
            scratch_shapes=[pltpu.VMEM((4 * rows, depth), BF16)],
        ),
        out_shape=[jax.ShapeDtypeStruct((rows, width), F32)]
        + [jax.ShapeDtypeStruct(*each) for each in sent],
        compiler_params=pltpu.CompilerParams(vmem_limit_bytes=40 << 20),
        cost_estimate=pl.CostEstimate(flops=1_000_000, bytes_accessed=1_000_000, transcendentals=0),
        name="down",
    )(td, *hidden, down_weight)


def per_device(tokens, gate_weight, up_weight, down_weight, block_ids, block_counts):
    d, t = lax.axis_index("dp"), lax.axis_index("tensor")
    td = (d ^ t).reshape(1).astype(jnp.int32)
    dt = jnp.stack([d ^ t, t]).astype(jnp.int32)
    active = active_units(block_ids, block_counts, gate_weight.shape[1])
    turn = [(a * 4 + b, b * 4 + a) for a in range(4) for b in range(4)]
    rows = tokens.shape[0] // 2
    swap = lambda x, axis, mask: lax.ppermute(x, axis, xor_perm(4, mask))
    after = lambda x, *earlier: lax.optimization_barrier((x, *earlier))[0]
    mine, blocks, keep, send, near, across, hidden, partial, got, outs = ({} for _ in range(10))
    kept, passed = {}, {}
    tick = [td]

    def turn_in(c):
        x = tokens[c * rows : (c + 1) * rows]
        mine[c] = lax.ppermute(x if c == 0 else after(x, mine[c - 1]), ("dp", "tensor"), turn)

    def spread(c):
        x = mine[c] if c == 0 else after(mine[c], *blocks[c - 1])
        two = swap(x, "tensor", 2)
        one = swap(after(x, two) if c == 0 else x, "tensor", 1)
        blocks[c] = [mine[c], one, two, swap(two, "tensor", 1)]

    def first(c):
        keep[c], *send[c] = gate_up(after(td, *tick), blocks[c], gate_weight, up_weight)
        tick[:] = send[c]

    def to_core(c, *earlier):
        held = lax.optimization_barrier((*send[c], *earlier))[:2] if earlier else send[c]
        near[c] = [swap(x, "dp", 1) for x in held]

    def to_chip(c):
        keep[c] = lax.optimization_barrier((keep[c], *tick))[0]
        summed = (keep[c][1] + near[c][1].astype(F32)).astype(BF16)
        across[c] = swap(summed, "dp", 2)
        tick[:] = [summed]

    def gated(c):
        x = after(keep[c], *tick)
        total = x[0] + near[c][0].astype(F32) + across[c].astype(F32)
        own = (jnp.maximum(total[0], 0.0) * total[1] * active).astype(BF16)
        far = swap(own, "dp", 2)
        hidden[c] = [own, swap(own, "dp", 1), far, swap(far, "dp", 1)]
        tick[:] = [own]

    def second(c, h, parts):
        stacked = parts == 1
        partial[c, h], *sent = down(after(dt, *tick), hidden[c], down_weight, h, parts, stacked)
        if stacked:
            arrived = lax.all_to_all(sent[0], "tensor", 0, 0, tiled=True)
            got[c, h] = [(arrived[j], t == j) for j in range(4)]
        else:
            kept[h] = sent[1]
            passed[h] = swap(sent[2], "tensor", 1)
            direct = after(sent[0], passed[h]) if h else sent[0]
            got[c, h] = [(swap(direct, "tensor", 1), None)]
        tick[:] = [sent[0]]

    def pass_on(c, h):
        summed = (after(kept[h], *tick) + passed[h].astype(F32)).astype(BF16)
        got[c, h].append((swap(summed, "tensor", 2), None))
        tick[:] = [summed]

    def mix(c, h):
        mixed = after(partial[c, h], *tick)
        for x, is_own in got[c, h]:
            x = x.astype(F32)
            mixed = mixed + (x if is_own is None else jnp.where(is_own, 0.0, x))
        mixed = mixed.astype(BF16)
        outs[c, h] = lax.ppermute(mixed, ("dp", "tensor"), turn)
        tick[:] = [mixed]

    turn_in(0)
    spread(0)
    turn_in(1)
    tick.append(mine[1])
    first(0)
    spread(1)
    to_core(0, *blocks[1][:3])
    to_chip(0)
    first(1)
    to_core(1)
    gated(0)
    to_chip(1)
    second(0, 0, 1)
    gated(1)
    second(1, 0, 2)
    mix(0, 0)
    second(1, 1, 2)
    pass_on(1, 0)
    pass_on(1, 1)
    mix(1, 0)
    mix(1, 1)
    last = jnp.concatenate([outs[1, 0], outs[1, 1]], axis=1)
    return jnp.concatenate([outs[0, 0], last], axis=0)


def per_device_general(tokens, gate_weight, up_weight, down_weight, block_ids, block_counts):
    gathered = lax.all_gather(tokens, "tensor", axis=1, tiled=True)
    turned = lax.all_to_all(gathered, "dp", 1, 0, tiled=True)
    active = active_units(block_ids, block_counts, gate_weight.shape[1])
    sums = [
        lax.psum_scatter(
            jnp.dot(turned, w, preferred_element_type=F32), "dp", scatter_dimension=0, tiled=True
        )
        for w in (gate_weight, up_weight)
    ]
    hidden = (jnp.maximum(sums[0], 0.0) * sums[1] * active).astype(BF16)
    hidden = lax.all_gather(hidden, "dp", axis=0, tiled=True)
    partial = jnp.dot(hidden, down_weight, preferred_element_type=F32)
    partial = lax.all_to_all(partial, "dp", 0, 1, tiled=True)
    return lax.psum_scatter(partial, "tensor", scatter_dimension=1, tiled=True).astype(BF16)


def solution(mesh):
    placed = (
        P(("groups", "dp"), "tensor"),
        P("dp", "tensor"),
        P("dp", "tensor"),
        P("tensor", "dp"),
        P(("groups", "tensor")),
        P(("groups", "tensor")),
    )
    square = mesh.shape["dp"] == 4 and mesh.shape["tensor"] == 4
    return jax.shard_map(
        per_device if square else per_device_general,
        mesh=mesh,
        in_specs=placed,
        out_specs=P(("groups", "dp"), "tensor"),
        check_vma=False,
    )
```
